256 devices in a mesh: dp: 4 (over x), expert: 64 (over z, y, core).
Axes of the slice: x: 4, y: 4, z: 8, core: 2. Of those that a mesh axis runs over, the one named last changes fastest.
Arguments:
- tokens: bfloat16 [32768, 4096], P(('dp', 'expert')), may hold values from -6 to 6
- grad_out: bfloat16 [32768, 4096], P(('dp', 'expert')), may hold values from -2 to 2
- gate_prob: float32 [32768], P(('dp', 'expert')), may hold values from 0.1 to 1
- expert_ids: int32 [32768, 1], P(('dp', 'expert')), may hold values from 0 to 63; in each aligned block of 128 rows (0 to 127, 128 to 255, ...) at most 3 rows name the same one
- w_in: bfloat16 [64, 4096, 1024], P('expert', 'dp'), may hold values from -0.09375 to 0.09375
- w_out: bfloat16 [64, 4096, 1024], P('expert', 'dp'), may hold values from -0.1875 to 0.1875
- threshold: float32 [64, 1024], P('expert'), may hold values from 0.25 to 1
- spike_counts: int32 [64, 768, 1024], P('expert', 'dp'), may hold values from 0 to 4
Outputs:
- token_grad: bfloat16 [32768, 4096], P(('dp', 'expert'))
- w_in_grad: bfloat16 [64, 4096, 1024], P('expert', 'dp')
- w_out_grad: bfloat16 [64, 4096, 1024], P('expert', 'dp')
The draws below stay inside these ranges and needn't reach their ends.
Inputs may be any that keep to these rules, and one draw needn't show every extreme that they name: `expert_ids`: in each device's block of 128 tokens no expert is chosen by more than 3 tokens, and some expert is chosen by exactly 3.
All inputs are finite; a program needn't handle non-finite values.
Results may differ from the reference program's by a relative error of at most 0.0057.
Values may be sent and summed in bfloat16 or wider, within the bound.
A program may use at most 128 MiB of HBM per device.

```python
import math
import jax
import jax.numpy as jnp
import numpy as np
from jax import lax

D = 4096
FF = 1024
STEPS = 4
TOK_DEV = 128
EXPERTS = 64
CAP = 3
TOKENS = 32768
ROWS_EXP = 768
N_DP = 4
N_EXPERT = 64


def touch_ends(array, rng, least, top_value):
    dims = array.shape
    spot = [jax.random.randint(jax.random.fold_in(rng, axis), (), 0, dims[axis]) for axis in range(len(dims))]
    array = array.at[tuple(spot)].set(least)
    longest = dims.index(max(dims))
    spot[longest] = (spot[longest] + 1) % dims[longest]
    return array.at[tuple(spot)].set(top_value)


def block_levels(key, shape, shards, low, high):
    def one(position, parts):
        steps = jax.random.uniform(jax.random.fold_in(jax.random.fold_in(key, 6), position), (parts,), jnp.float32, low / len(shards), high / len(shards))
        return jnp.repeat(jnp.exp(steps), shape[position] // parts).reshape((-1,) + (1,) * (len(shape) - position - 1))

    loudness = one(*shards[0])
    for cut in shards[1:]:
        loudness = loudness * one(*cut)
    return loudness


def shared_out(stream_key, own, number, rows, count, top, bound, skew):
    ranking = jax.random.permutation(stream_key, count)
    heavy_load, usual = shares(count, rows * top, bound, skew, True), shares(count, rows * top, bound, skew, False)
    places = jnp.arange(count)

    def named(sizes, offset_by):
        used = int((sizes > 0).sum())
        fixed = max(1, used // 4)
        moved = fixed + (places - fixed + offset_by * (used - fixed)) % max(1, count - fixed)
        return jnp.zeros((count,), jnp.int32).at[ranking[jnp.where(places < fixed, places, moved)]].set(jnp.asarray(sizes, jnp.int32))

    sizes = jnp.where(number % 4 == 0, named(heavy_load, number // 4), named(usual, number - number // 4 - 1))
    mixed = jax.random.permutation(jax.random.fold_in(own, 3), count)
    source_of, sink = mixed[0:count // 2 * 2:2], mixed[1:count // 2 * 2:2]
    margin = jnp.minimum(sizes[source_of] - 1, bound - sizes[sink]) // 2
    margin = jnp.where((source_of == ranking[0]) | (sink == ranking[0]) | (sizes[sink] == 0), 0, jnp.maximum(margin, 0))
    moved = jax.random.randint(jax.random.fold_in(own, 4), (count // 2,), 0, 1 << 20) % (margin + 1)
    sizes = sizes.at[source_of].add(-moved).at[sink].add(moved)
    members = jnp.searchsorted(jnp.cumsum(sizes), jnp.arange(rows * top), side="right").astype(jnp.int32)
    grid = members.reshape(top, rows).T
    grid = grid[jax.random.permutation(jax.random.fold_in(own, 1), rows)]
    offset_by = jax.random.randint(jax.random.fold_in(own, 2), (rows, 1), 0, top)
    return jnp.take_along_axis(grid, (jnp.arange(top)[None, :] + offset_by) % top, axis=1)


def shares(count, total, most, slope, full):
    portions = [(1 << 20) // math.isqrt(rank ** slope) + 1 for rank in range(1, count + 1)]
    largest = most if full else min(most, max(-(-total // count), total * portions[0] // sum(portions)))
    least = 1 if total - largest >= count - 1 else 0
    holding, rest = [largest] + [least] * (count - 1), total - largest - least * (count - 1)
    while rest > 0:
        free = [i for i in range(1, count) if holding[i] < largest] or [i for i in range(1, count) if holding[i] < most]
        whole, budget = sum([portions[i] for i in free]), rest
        for i in free:
            addition = min(most - holding[i], max(1, budget * portions[i] // whole), rest)
            holding[i] = holding[i] + addition
            rest = rest - addition
    return np.array(holding)


def bell_draw(key, dims, width, bound, pieces=(), kind=jnp.bfloat16):
    loudness = block_levels(key, dims, pieces, -0.22, 0.18) if pieces else 1.0
    values = jax.random.normal(key, dims, jnp.float32) * width * loudness
    return jnp.minimum(jnp.maximum(values, -bound), bound).astype(kind)


def setup_inputs(seed: int = 0) -> dict:
    seeds = jax.random.split(jax.random.key(seed), 9)
    tokens = bell_draw(seeds[0], (TOKENS, D), 1.0, 6.0, ((0, 256),))
    grad_out = bell_draw(seeds[1], (TOKENS, D), 0.3, 2.0, ((0, 256),))
    gate_prob = jnp.clip(jnp.exp(math.log(1.0) - 2.3025851 * jax.random.uniform(seeds[2], (TOKENS,), jnp.float32) ** block_levels(seeds[2], (TOKENS,), ((0, 256),), -0.2, 0.2)), 0.1, 1.0)
    expert_ids_keys = jax.random.split(jax.random.fold_in(seeds[3], 1), TOKENS // TOK_DEV)
    expert_ids_turns = jax.random.permutation(jax.random.fold_in(seeds[3], 3), TOKENS // TOK_DEV)
    expert_ids = jax.vmap(lambda own, number: shared_out(jax.random.fold_in(seeds[3], 2), own, number, TOK_DEV, EXPERTS, 1, CAP, 2))(expert_ids_keys, expert_ids_turns).reshape((TOKENS, 1))
    w_in = bell_draw(seeds[4], (EXPERTS, D, FF), D ** -0.5, 0.09375, ((0, 64), (1, 4)))
    w_out = bell_draw(seeds[5], (EXPERTS, D, FF), FF ** -0.5, 0.1875, ((0, 64), (1, 4)))
    threshold = jnp.clip(jnp.exp(math.log(1.0) - 1.3862944 * jax.random.uniform(seeds[6], (EXPERTS, FF), jnp.float32) ** block_levels(seeds[6], (EXPERTS, FF), ((0, 64),), -0.2, 0.2)), 0.25, 1.0)
    spike_counts = touch_ends(jax.random.randint(seeds[7], (EXPERTS, ROWS_EXP, FF), 0, STEPS + 1), jax.random.fold_in(seeds[7], 1), 0, STEPS).astype(jnp.int32)
    return dict(tokens=tokens, grad_out=grad_out, gate_prob=gate_prob, expert_ids=expert_ids, w_in=w_in, w_out=w_out, threshold=threshold, spike_counts=spike_counts)


sharpness = 4.0


def selection(block_ids, expert_count, capacity):
    onehot = (block_ids[:, None] == jnp.arange(expert_count, dtype=jnp.int32)[None, :]).astype(jnp.int32)
    before = jnp.cumsum(onehot, axis=0) - onehot
    slot = jnp.sum(onehot * before, axis=1).astype(jnp.int32)
    place = block_ids * capacity + slot
    targets = jnp.arange(expert_count * capacity, dtype=jnp.int32)
    return (targets[:, None] == place[None, :]).astype(jnp.bfloat16)


def surrogate(membrane, limit):
    total = jnp.zeros_like(membrane)
    for step in range(STEPS):
        shifted = sharpness * (membrane - (step + 0.5) * limit[None, :])
        sig = jax.nn.sigmoid(shifted)
        total = total + sharpness * sig * (1.0 - sig)
    return total


def reference(tokens, grad_out, gate_prob, expert_ids, w_in, w_out, threshold, spike_counts):
    blocks = N_DP * N_EXPERT
    scaled = (gate_prob[:, None] * grad_out.astype(jnp.float32)).astype(jnp.bfloat16)
    block_ids = expert_ids[:, 0].reshape(blocks, TOK_DEV)
    selects = jax.vmap(lambda b: selection(b, EXPERTS, CAP))(block_ids)
    x_blocks = tokens.reshape(blocks, TOK_DEV, D)
    g_blocks = scaled.reshape(blocks, TOK_DEV, D)

    def dispatch(item):
        sel, xb, gb = item
        sx = jnp.dot(sel, xb, preferred_element_type=jnp.float32).astype(jnp.bfloat16)
        sg = jnp.dot(sel, gb, preferred_element_type=jnp.float32).astype(jnp.bfloat16)
        return sx, sg

    send_x, send_g = lax.map(dispatch, (selects, x_blocks, g_blocks))
    routed_x = send_x.reshape(N_DP, N_EXPERT, EXPERTS, CAP, D).transpose(2, 0, 1, 3, 4).reshape(EXPERTS, ROWS_EXP, D)
    routed_g = send_g.reshape(N_DP, N_EXPERT, EXPERTS, CAP, D).transpose(2, 0, 1, 3, 4).reshape(EXPERTS, ROWS_EXP, D)

    def per_expert(item):
        rx, rg, win, wout, limit, counts = item
        membrane = jnp.dot(rx, win, preferred_element_type=jnp.float32)
        upstream = lax.dot_general(rg, wout, (((1,), (0,)), ((), ())), preferred_element_type=jnp.float32)
        grad_hidden = (upstream * surrogate(membrane, limit)).astype(jnp.bfloat16)
        activity = (limit[None, :] * counts.astype(jnp.float32) / STEPS).astype(jnp.bfloat16)
        slot_grad = lax.dot_general(grad_hidden, win, (((1,), (1,)), ((), ())), preferred_element_type=jnp.float32).astype(jnp.bfloat16)
        gin = lax.dot_general(rx, grad_hidden, (((0,), (0,)), ((), ())), preferred_element_type=jnp.float32).astype(jnp.bfloat16)
        gout = lax.dot_general(rg, activity, (((0,), (0,)), ((), ())), preferred_element_type=jnp.float32).astype(jnp.bfloat16)
        return slot_grad, gin, gout

    slot_grad, w_in_grad, w_out_grad = lax.map(per_expert, (routed_x, routed_g, w_in, w_out, threshold, spike_counts))
    back = slot_grad.reshape(EXPERTS, N_DP, N_EXPERT, CAP, D).transpose(1, 2, 0, 3, 4).reshape(blocks, EXPERTS * CAP, D)

    def combine(item):
        sel, buf = item
        return lax.dot_general(sel, buf, (((0,), (0,)), ((), ())), preferred_element_type=jnp.float32).astype(jnp.bfloat16)

    token_grad = lax.map(combine, (selects, back)).reshape(TOKENS, D)
    return token_grad, w_in_grad, w_out_grad
```

```python
import functools
import jax
import jax.numpy as jnp
from jax import lax
from jax.experimental import pallas as pl
from jax.experimental.pallas import tpu as pltpu
from jax.sharding import PartitionSpec as P

STEPS = 4
SHARP = 4.0
TOK = 128
CAP = 3
NE = 64
ND = 4
W = 1024
FF = 1024
HALF = 512
MAIN = 384
PIECE = 128
NC = 4
KC = 16
ROWS = 192
HOME = 48
MROWS = KC * 16
F32, BF16, I32 = jnp.float32, jnp.bfloat16, jnp.int32
MESH = pl.DeviceIdType.MESH


def dot(a, b, dims=((1,), (0,))):
    return lax.dot_general(a, b, (dims, ((), ())), preferred_element_type=F32)


def one_hot(cond):
    return jnp.where(cond, 1.0, 0.0).astype(BF16)


def row_parts(p):
    rr = (p >= 48).astype(I32) + (p >= 96).astype(I32) + (p >= 144).astype(I32)
    pp = p - 48 * rr
    kk = (pp * 171) >> 9
    return rr, kk, pp - 3 * kk


def spread(p, q, m):
    rr, kk, c3 = row_parts(p)
    rho = rr * 3 + c3
    if m is None:
        return q == kk * 16 + rho
    return (q == kk * 16 + 12 + (rho & 3)) & ((rho >> 2) == m)


def kernel(
    gate, ids, limit, tokens, grads, w_in, w_out, spikes,
    tok_out, win_out, wout_out,
    grad_v, scaled, spike_v, win_v, wout_v, pos_v, xin, sel0, sel1, p0, p1, pt0, pt1,
    fsend, frecv, rows, msend, mrecv, uown, usend, urecv, hid, act, rsend, rrecv, tsend, wg,
    lsem, pos_s, pos_r, x_s, x_r, f_s, f_r, m_s, m_r, u_s, u_r, h_s, h_r, a_s, a_r, r_s, r_r, t_s, t_r, w_s,
):
    r = lax.axis_index("dp")
    e = lax.axis_index("expert")
    z, y, c = e // 8, (e // 2) % 4, e % 2

    def there(k):
        dy, dz, dc = k // 16, (k // 2) % 8, k % 2
        return (r, ((z + dz) % 8) * 8 + ((y + dy) % 4) * 2 + (c + dc) % 2)

    def back(k):
        dy, dz, dc = k // 16, (k // 2) % 8, k % 2
        return (r, ((z + 8 - dz) % 8) * 8 + ((y + 4 - dy) % 4) * 2 + (c + dc) % 2)

    def replica(d):
        return (r + d) % ND

    def remote(src, dst, ss, rs, device):
        return pltpu.make_async_remote_copy(
            src_ref=src, dst_ref=dst, send_sem=ss, recv_sem=rs, device_id=device, device_id_type=MESH
        )

    def arrived(ref, ss, rs):
        remote(ref, ref, ss, rs, (replica(1), e)).wait_recv()

    def sent(ref, ss, rs):
        remote(ref, ref, ss, rs, (replica(1), e)).wait_send()

    def order(i):
        dzi = i // 2
        half = dzi // 2
        return (half + (dzi % 2) * (7 - 2 * half)) * 2 + i % 2

    load_g = pltpu.make_async_copy(grads, grad_v, lsem.at[0])
    load_g.start()
    load_in = pltpu.make_async_copy(w_in, win_v, lsem.at[1])
    load_in.start()
    load_out = pltpu.make_async_copy(w_out, wout_v, lsem.at[2])
    load_out.start()
    load_s = pltpu.make_async_copy(spikes, spike_v, lsem.at[3])
    load_s.start()

    barrier = pltpu.get_barrier_semaphore()

    @pl.loop(1, NE)
    def _(k):
        pl.semaphore_signal(barrier, inc=1, device_id=there(k), device_id_type=MESH)

    for d in range(1, ND):
        pl.semaphore_signal(barrier, inc=1, device_id=(replica(d), e), device_id_type=MESH)

    col = ids[...]
    ti = lax.broadcasted_iota(I32, (TOK, TOK), 0)
    tj = lax.broadcasted_iota(I32, (TOK, TOK), 1)
    row = jnp.sum(jnp.where(ti == tj, col, 0), axis=0, keepdims=True)
    slot = jnp.sum(jnp.where((col == row) & (ti < tj), 1, 0), axis=0, keepdims=True)
    kidx = ((((row >> 1) & 3) - y) & 3) * 16 + (((row >> 3) - z) & 7) * 2 + ((row & 1) ^ c)
    pos = kidx * 16 + r * CAP + slot
    pos_v[r] = jnp.broadcast_to(pos, (8, TOK))

    pl.semaphore_wait(barrier, NE - 1 + ND - 1)

    for d in (2, 1, 3):
        remote(pos_v.at[r], pos_v.at[r], pos_s, pos_r, (replica(d), e)).start()

    def exchange(a, h, source):
        mine = xin.at[a, pl.ds(pl.multiple_of(r * TOK, TOK), TOK), pl.ds(h * HALF, HALF)]

        def piece(q):
            return source.at[:, pl.ds(pl.multiple_of(q * W + h * HALF, HALF), HALF)]

        pltpu.make_async_copy(piece(r), mine, x_r.at[a, h]).start()
        for d in (2, 1, 3):
            remote(piece(replica(d)), mine, x_s.at[a, h], x_r.at[a, h], (replica(d), e)).start()

    exchange(0, 0, tokens)
    exchange(0, 1, tokens)

    load_g.wait()
    gate_col = jnp.sum(jnp.where(ti == tj, gate[...], 0.0), axis=1, keepdims=True)

    @pl.loop(0, 8)
    def _(i):
        cols = pl.ds(pl.multiple_of(i * 512, 512), 512)
        scaled[:, cols] = (gate_col * grad_v[:, cols].astype(F32)).astype(BF16)

    pi = lax.broadcasted_iota(I32, (ROWS, MROWS), 0)
    qi = lax.broadcasted_iota(I32, (ROWS, MROWS), 1)
    p0[...] = one_hot(spread(pi, qi, None))
    for m in range(3):
        p1[m] = one_hot(spread(pi, qi, m))
    pi = lax.broadcasted_iota(I32, (MROWS, ROWS), 1)
    qi = lax.broadcasted_iota(I32, (MROWS, ROWS), 0)
    pt0[...] = one_hot(spread(pi, qi, None))
    for m in range(3):
        pt1[m] = one_hot(spread(pi, qi, m))

    arrived(pos_v.at[pl.ds(0, 3)], pos_s, pos_r)

    @pl.loop(0, NC)
    def _(ch):
        base = ch * MROWS
        qi = lax.broadcasted_iota(I32, (MROWS, TOK), 0) + base
        at = pl.ds(pl.multiple_of(base, MROWS), MROWS)
        for q in range(ND):
            where = pos_v[q][0:1]
            rho = where & 15
            tail = where - rho + 12 + (rho & 3)
            cols = slice(q * TOK, (q + 1) * TOK)
            sel0[at, cols] = one_hot(qi == where)
            for m in range(3):
                sel1[m, at, cols] = one_hot(qi == jnp.where((rho >> 2) == m, tail, -1))

    def select(a, h, ch):
        at = pl.ds(pl.multiple_of(ch * MROWS, MROWS), MROWS)
        main = dot(sel0[at, :], xin[a, :, h * HALF : h * HALF + MAIN])
        tail = xin[a, :, h * HALF + MAIN : (h + 1) * HALF]
        for m in range(3):
            cols = slice(m * PIECE, (m + 1) * PIECE)
            both = main[:, cols] + dot(sel1[m, at, :], tail)
            fsend[a, pl.ds(ch * KC, KC), h, :, cols] = both.astype(BF16).reshape(KC, 16, PIECE)

    def deliver(ch, src, dst, ss, rs, target):
        @pl.loop(0, KC)
        def _(i):
            k = ch * KC + order(i)

            @pl.when(k == 0)
            def _():
                pltpu.make_async_copy(src(k), dst(k), rs).start()

            @pl.when(k != 0)
            def _():
                remote(src(k), dst(k), ss, rs, target(k)).start()

    for h in range(2):
        arrived(xin.at[0, :, pl.ds(h * HALF, HALF)], x_s.at[0, h], x_r.at[0, h])

        @pl.loop(0, NC)
        def _(ch):
            select(0, h, ch)
            deliver(
                ch, lambda k: fsend.at[0, k, h], lambda k: frecv.at[0, k, h], f_s.at[0], f_r.at[h * NC + ch], there
            )

        if h == 0:
            exchange(1, 0, scaled)
            exchange(1, 1, scaled)

    load_s.wait()
    pi = lax.broadcasted_iota(I32, (ROWS, ROWS), 0)
    qi = lax.broadcasted_iota(I32, (ROWS, ROWS), 1)
    dy, kk, c3 = row_parts(pi)
    origin = (((z - (kk >> 1)) & 7) * 8 + ((y - dy) & 3) * 2 + (c ^ (kk & 1))) * CAP + c3
    natural = (limit[...] * spike_v[...].astype(F32) / STEPS).astype(BF16)
    ordered = dot(one_hot(qi == origin), natural).astype(BF16)
    for ch in range(NC):
        act[ch, r] = ordered[ch * HOME : (ch + 1) * HOME]

    for h in range(2):
        arrived(xin.at[1, :, pl.ds(h * HALF, HALF)], x_s.at[1, h], x_r.at[1, h])

    @pl.loop(0, NC)
    def _(ch):
        select(1, 0, ch)
        select(1, 1, ch)
        deliver(ch, lambda k: fsend.at[1, k], lambda k: frecv.at[1, k], f_s.at[1], f_r.at[2 * NC + ch], there)

    for d in (2, 1, 3):
        remote(act.at[:, r], act.at[:, r], a_s, a_r, (replica(d), e)).start()

    load_in.wait()
    load_out.wait()

    def compact(a, ch):
        at = pl.ds(pl.multiple_of(ch * ROWS, ROWS), ROWS)
        for h in range(2):
            block = frecv[a, pl.ds(ch * KC, KC), h].reshape(MROWS, MAIN)
            rows[a, at, h * HALF : h * HALF + MAIN] = dot(p0[...], block).astype(BF16)
            tail = sum(dot(p1[m], block[:, m * PIECE : (m + 1) * PIECE]) for m in range(3))
            rows[a, at, h * HALF + MAIN : (h + 1) * HALF] = tail.astype(BF16)
        return rows[a, at, :]

    @pl.loop(0, NC)
    def _(ch):
        arrived(frecv.at[0, pl.ds(ch * KC, KC), 0], f_s.at[0], f_r.at[ch])
        arrived(frecv.at[0, pl.ds(ch * KC, KC), 1], f_s.at[0], f_r.at[NC + ch])
        msend[ch] = dot(compact(0, ch), win_v[...]).reshape(ND, HOME, FF)
        for d in (2, 1, 3):
            q = replica(d)
            remote(msend.at[ch, q], mrecv.at[ch, d - 1], m_s, m_r.at[ch], (q, e)).start()

    def upstream(ch):
        arrived(frecv.at[1, pl.ds(ch * KC, KC)], f_s.at[1], f_r.at[2 * NC + ch])
        part = dot(compact(1, ch), wout_v[...]).reshape(ND, HOME, FF)
        uown[...] = part
        usend[ch] = part.astype(BF16)
        for d in (2, 1, 3):
            q = replica(d)
            remote(usend.at[ch, q], urecv.at[ch, d - 1], u_s, u_r.at[ch], (q, e)).start()

    def hidden(ch):
        arrived(mrecv.at[ch], m_s, m_r.at[ch])
        arrived(urecv.at[ch], u_s, u_r.at[ch])

        @pl.loop(0, 3)
        def _(i):
            at = pl.ds(pl.multiple_of(i * 16, 16), 16)
            membrane = msend[ch, r, at] + mrecv[ch, 0, at] + mrecv[ch, 1, at] + mrecv[ch, 2, at]
            up = uown[r, at]
            for d in range(3):
                up = up + urecv[ch, d, at].astype(F32)
            total = jnp.zeros_like(membrane)
            for step in range(STEPS):
                sig = jax.nn.sigmoid(SHARP * (membrane - (step + 0.5) * limit[...]))
                total = total + SHARP * sig * (1.0 - sig)
            hid[ch, r, at] = (up * total).astype(BF16)

        for d in (2, 1, 3):
            remote(hid.at[ch, r], hid.at[ch, r], h_s, h_r.at[ch], (replica(d), e)).start()

    def slot_grad(ch):
        arrived(hid.at[ch, pl.ds(0, 3)], h_s, h_r.at[ch])
        sg = dot(hid[ch].reshape(ROWS, FF), win_v[...], ((1,), (1,))).astype(BF16)
        for h in range(2):
            main = dot(pt0[...], sg[:, h * HALF : h * HALF + MAIN])
            tail = sg[:, h * HALF + MAIN : (h + 1) * HALF]
            for m in range(3):
                cols = slice(m * PIECE, (m + 1) * PIECE)
                both = main[:, cols] + dot(pt1[m], tail)
                rsend[h, pl.ds(ch * KC, KC), :, cols] = both.astype(BF16).reshape(KC, 16, PIECE)

    def give_back(h, ch):
        deliver(ch, lambda k: rsend.at[h, k], lambda k: rrecv.at[h, k], r_s.at[h], r_r.at[h], back)

    @pl.loop(0, NC)
    def _(ch):
        upstream(ch)

        @pl.when(ch > 0)
        def _():
            slot_grad(ch - 1)
            give_back(0, ch - 1)

        hidden(ch)

    def weight_grad(a, right, out):
        @pl.loop(0, 4)
        def _(i):
            at = pl.ds(pl.multiple_of(i * 256, 256), 256)
            wg[a, at, :] = dot(rows[a, :, at], right[...].reshape(NC * ROWS, FF), ((0,), (0,))).astype(BF16)

        pltpu.make_async_copy(wg.at[a], out, w_s.at[a]).start()

    slot_grad(NC - 1)
    give_back(0, NC - 1)

    @pl.loop(0, NC)
    def _(ch):
        give_back(1, ch)

    weight_grad(0, hid, win_out)
    arrived(act.at[:, pl.ds(0, 3)], a_s, a_r)
    weight_grad(1, act, wout_out)

    for h in range(2):
        arrived(rrecv.at[h], r_s.at[h], r_r.at[h])
        block = rrecv[h].reshape(NC * MROWS, MAIN)
        tsend[h, :, 0:MAIN] = dot(sel0[...], block, ((0,), (0,))).astype(BF16)
        tail = sum(dot(sel1[m], block[:, m * PIECE : (m + 1) * PIECE], ((0,), (0,))) for m in range(3))
        tsend[h, :, MAIN:HALF] = tail.astype(BF16)
        place = tok_out.at[:, pl.ds(pl.multiple_of(r * W + h * HALF, HALF), HALF)]

        def part(q):
            return tsend.at[h, pl.ds(pl.multiple_of(q * TOK, TOK), TOK)]

        pltpu.make_async_copy(part(r), place, t_r.at[h]).start()
        for d in (2, 1, 3):
            q = replica(d)
            remote(part(q), place, t_s.at[h], t_r.at[h], (q, e)).start()

    sent(pos_v.at[pl.ds(0, 3)], pos_s, pos_r)
    for a in range(2):
        for h in range(2):
            sent(xin.at[a, pl.ds(0, 3 * TOK), pl.ds(h * HALF, HALF)], x_s.at[a, h], x_r.at[a, h])
        sent(fsend.at[a, pl.ds(1, NE - 1)], f_s.at[a], f_r.at[0])
    sent(msend.at[pl.ds(0, 3)], m_s, m_r.at[0])
    sent(usend.at[pl.ds(0, 3)], u_s, u_r.at[0])
    sent(hid.at[pl.ds(0, 3)], h_s, h_r.at[0])
    sent(act.at[:, pl.ds(0, 3)], a_s, a_r)
    for h in range(2):
        sent(rsend.at[h, pl.ds(1, NE - 1)], r_s.at[h], r_r.at[h])
        sent(tsend.at[h, pl.ds(0, 3 * TOK)], t_s.at[h], t_r.at[h])
    for a, out in enumerate((win_out, wout_out)):
        pltpu.make_async_copy(wg.at[a], out, w_s.at[a]).wait()
    for h in range(2):
        arrived(tok_out.at[:, pl.ds(0, ND * HALF)], t_s.at[h], t_r.at[h])


def on_device(tokens, grad_out, gate_prob, expert_ids, w_in, w_out, threshold, spike_counts):
    vmem = pl.BlockSpec(memory_space=pltpu.VMEM)
    hbm = pl.BlockSpec(memory_space=pl.ANY)
    dma = pltpu.SemaphoreType.DMA
    out = pl.pallas_call(
        kernel,
        name="moe_backward",
        out_shape=(
            jax.ShapeDtypeStruct((TOK, ND * W), BF16),
            jax.ShapeDtypeStruct((W, FF), BF16),
            jax.ShapeDtypeStruct((W, FF), BF16),
        ),
        in_specs=[vmem, vmem, vmem] + [hbm] * 5,
        out_specs=(hbm, hbm, hbm),
        scratch_shapes=[
            pltpu.VMEM((TOK, ND * W), BF16),
            pltpu.VMEM((TOK, ND * W), BF16),
            pltpu.VMEM((ROWS, FF), I32),
            pltpu.VMEM((W, FF), BF16),
            pltpu.VMEM((W, FF), BF16),
            pltpu.VMEM((ND, 8, TOK), I32),
            pltpu.VMEM((2, ND * TOK, W), BF16),
            pltpu.VMEM((NC * MROWS, ND * TOK), BF16),
            pltpu.VMEM((3, NC * MROWS, ND * TOK), BF16),
            pltpu.VMEM((ROWS, MROWS), BF16),
            pltpu.VMEM((3, ROWS, MROWS), BF16),
            pltpu.VMEM((MROWS, ROWS), BF16),
            pltpu.VMEM((3, MROWS, ROWS), BF16),
            pltpu.VMEM((2, NE, 2, 16, MAIN), BF16),
            pltpu.VMEM((2, NE, 2, 16, MAIN), BF16),
            pltpu.VMEM((2, NC * ROWS, W), BF16),
            pltpu.VMEM((NC, ND, HOME, FF), F32),
            pltpu.VMEM((NC, 3, HOME, FF), F32),
            pltpu.VMEM((ND, HOME, FF), F32),
            pltpu.VMEM((NC, ND, HOME, FF), BF16),
            pltpu.VMEM((NC, 3, HOME, FF), BF16),
            pltpu.VMEM((NC, ND, HOME, FF), BF16),
            pltpu.VMEM((NC, ND, HOME, FF), BF16),
            pltpu.VMEM((2, NE, 16, MAIN), BF16),
            pltpu.VMEM((2, NE, 16, MAIN), BF16),
            pltpu.VMEM((2, ND * TOK, HALF), BF16),
            pltpu.VMEM((2, W, FF), BF16),
            dma((4,)),
            dma, dma,
            dma((2, 2)), dma((2, 2)),
            dma((2,)), dma((3 * NC,)),
            dma, dma((NC,)),
            dma, dma((NC,)),
            dma, dma((NC,)),
            dma, dma,
            dma((2,)), dma((2,)),
            dma((2,)), dma((2,)),
            dma((2,)),
        ],
        compiler_params=pltpu.CompilerParams(
            collective_id=0, has_side_effects=True, vmem_limit_bytes=58 << 20
        ),
        cost_estimate=pl.CostEstimate(flops=9 * 10**9, bytes_accessed=14 << 20, transcendentals=1 << 20),
    )(
        gate_prob.reshape(1, TOK), expert_ids, threshold, tokens, grad_out,
        w_in.reshape(W, FF), w_out.reshape(W, FF), spike_counts.reshape(ROWS, FF),
    )
    return out[0], out[1][None], out[2][None]


def solution(mesh):
    placed = (
        P(("dp", "expert"), None),
        P(("dp", "expert"), None),
        P(("dp", "expert")),
        P(("dp", "expert"), None),
        P("expert", "dp", None),
        P("expert", "dp", None),
        P("expert", None),
        P("expert", "dp", None),
    )
    return jax.shard_map(
        on_device,
        mesh=mesh,
        in_specs=placed,
        out_specs=(P(("dp", "expert"), None), P("expert", "dp", None), P("expert", "dp", None)),
        check_vma=False,
    )
```

```python
import functools
import jax
import jax.numpy as jnp
from jax import lax
from jax.experimental import pallas as pl
from jax.experimental.pallas import tpu as pltpu
from jax.sharding import PartitionSpec as P

STEPS = 4
SHARP = 4.0
TOK = 128
CAP = 3
NE = 64
ND = 4
W = 1024
FF = 1024
HALF = 512
MAIN = 384
PIECE = 128
NC = 4
KC = 16
ROWS = 192
HOME = 48
MROWS = KC * 16
F32, BF16, I32 = jnp.float32, jnp.bfloat16, jnp.int32
MESH = pl.DeviceIdType.MESH


def dot(a, b, dims=((1,), (0,))):
    return lax.dot_general(a, b, (dims, ((), ())), preferred_element_type=F32)


def one_hot(cond):
    return jnp.where(cond, 1.0, 0.0).astype(BF16)


def row_parts(p):
    rr = (p >= 48).astype(I32) + (p >= 96).astype(I32) + (p >= 144).astype(I32)
    pp = p - 48 * rr
    kk = (pp * 171) >> 9
    return rr, kk, pp - 3 * kk


def spread(p, q, m):
    rr, kk, c3 = row_parts(p)
    rho = rr * 3 + c3
    if m is None:
        return q == kk * 16 + rho
    return (q == kk * 16 + 12 + (rho & 3)) & ((rho >> 2) == m)


def kernel(
    gate, ids, limit, tokens, grads, w_in, w_out, spikes,
    tok_out, win_out, wout_out,
    grad_v, scaled, spike_v, win_v, wout_v, pos_v, xin, sel0, sel1, p0, p1, pt0, pt1,
    fsend, frecv, rows, msend, mrecv, uown, usend, urecv, hid, act, rsend, rrecv, tsend, wg,
    lsem, pos_s, pos_r, x_s, x_r, f_s, f_r, m_s, m_r, u_s, u_r, h_s, h_r, a_s, a_r, r_s, r_r, t_s, t_r, w_s,
):
    r = lax.axis_index("dp")
    e = lax.axis_index("expert")
    z, y, c = e // 8, (e // 2) % 4, e % 2

    def there(k):
        dy, dz, dc = k // 16, (k // 2) % 8, k % 2
        return (r, ((z + dz) % 8) * 8 + ((y + dy) % 4) * 2 + (c + dc) % 2)

    def back(k):
        dy, dz, dc = k // 16, (k // 2) % 8, k % 2
        return (r, ((z + 8 - dz) % 8) * 8 + ((y + 4 - dy) % 4) * 2 + (c + dc) % 2)

    def replica(d):
        return (r + d) % ND

    def remote(src, dst, ss, rs, device):
        return pltpu.make_async_remote_copy(
            src_ref=src, dst_ref=dst, send_sem=ss, recv_sem=rs, device_id=device, device_id_type=MESH
        )

    def arrived(ref, ss, rs):
        remote(ref, ref, ss, rs, (replica(1), e)).wait_recv()

    def sent(ref, ss, rs):
        remote(ref, ref, ss, rs, (replica(1), e)).wait_send()

    def order(i):
        dzi = i // 2
        half = dzi // 2
        return (half + (dzi % 2) * (7 - 2 * half)) * 2 + i % 2

    load_g = pltpu.make_async_copy(grads, grad_v, lsem.at[0])
    load_g.start()
    load_in = pltpu.make_async_copy(w_in, win_v, lsem.at[1])
    load_in.start()
    load_out = pltpu.make_async_copy(w_out, wout_v, lsem.at[2])
    load_out.start()
    load_s = pltpu.make_async_copy(spikes, spike_v, lsem.at[3])
    load_s.start()

    barrier = pltpu.get_barrier_semaphore()

    @pl.loop(1, NE)
    def _(k):
        pl.semaphore_signal(barrier, inc=1, device_id=there(k), device_id_type=MESH)

    for d in range(1, ND):
        pl.semaphore_signal(barrier, inc=1, device_id=(replica(d), e), device_id_type=MESH)

    row = ids[...]
    ti = lax.broadcasted_iota(I32, (TOK, TOK), 0)
    tj = lax.broadcasted_iota(I32, (TOK, TOK), 1)
    col = jnp.sum(jnp.where(ti == tj, row, 0), axis=1, keepdims=True)
    slot = jnp.sum(jnp.where((col == row) & (ti < tj), 1, 0), axis=0, keepdims=True)
    kidx = ((((row >> 1) & 3) - y) & 3) * 16 + (((row >> 3) - z) & 7) * 2 + ((row & 1) ^ c)
    pos = kidx * 16 + r * CAP + slot
    pos_v[r] = jnp.broadcast_to(pos, (8, TOK))

    pl.semaphore_wait(barrier, NE - 1 + ND - 1)

    for d in (2, 1, 3):
        remote(pos_v.at[r], pos_v.at[r], pos_s, pos_r, (replica(d), e)).start()

    def exchange(a, h, source):
        mine = xin.at[a, pl.ds(pl.multiple_of(r * TOK, TOK), TOK), pl.ds(h * HALF, HALF)]

        def piece(q):
            return source.at[:, pl.ds(pl.multiple_of(q * W + h * HALF, HALF), HALF)]

        pltpu.make_async_copy(piece(r), mine, x_r.at[a, h]).start()
        for d in (2, 1, 3):
            remote(piece(replica(d)), mine, x_s.at[a, h], x_r.at[a, h], (replica(d), e)).start()

    exchange(0, 0, tokens)

    load_g.wait()
    gate_col = jnp.sum(jnp.where(ti == tj, gate[...], 0.0), axis=1, keepdims=True)

    @pl.loop(0, 8)
    def _(i):
        cols = pl.ds(pl.multiple_of(i * 512, 512), 512)
        scaled[:, cols] = (gate_col * grad_v[:, cols].astype(F32)).astype(BF16)

    exchange(0, 1, tokens)

    pi = lax.broadcasted_iota(I32, (ROWS, MROWS), 0)
    qi = lax.broadcasted_iota(I32, (ROWS, MROWS), 1)
    p0[...] = one_hot(spread(pi, qi, None))
    for m in range(3):
        p1[m] = one_hot(spread(pi, qi, m))
    pi = lax.broadcasted_iota(I32, (MROWS, ROWS), 1)
    qi = lax.broadcasted_iota(I32, (MROWS, ROWS), 0)
    pt0[...] = one_hot(spread(pi, qi, None))
    for m in range(3):
        pt1[m] = one_hot(spread(pi, qi, m))

    arrived(pos_v.at[pl.ds(0, 3)], pos_s, pos_r)

    @pl.loop(0, NC)
    def _(ch):
        base = ch * MROWS
        qi = lax.broadcasted_iota(I32, (MROWS, TOK), 0) + base
        at = pl.ds(pl.multiple_of(base, MROWS), MROWS)
        for q in range(ND):
            where = pos_v[q][0:1]
            rho = where & 15
            tail = where - rho + 12 + (rho & 3)
            cols = slice(q * TOK, (q + 1) * TOK)
            sel0[at, cols] = one_hot(qi == where)
            for m in range(3):
                sel1[m, at, cols] = one_hot(qi == jnp.where((rho >> 2) == m, tail, -1))

    def select(a, h, ch):
        at = pl.ds(pl.multiple_of(ch * MROWS, MROWS), MROWS)
        main = dot(sel0[at, :], xin[a, :, h * HALF : h * HALF + MAIN])
        tail = xin[a, :, h * HALF + MAIN : (h + 1) * HALF]
        for m in range(3):
            cols = slice(m * PIECE, (m + 1) * PIECE)
            both = main[:, cols] + dot(sel1[m, at, :], tail)
            fsend[a, pl.ds(ch * KC, KC), h, :, cols] = both.astype(BF16).reshape(KC, 16, PIECE)

    def deliver(ch, src, dst, ss, rs, target):
        @pl.loop(0, KC)
        def _(i):
            k = ch * KC + order(i)

            @pl.when(k == 0)
            def _():
                pltpu.make_async_copy(src(k), dst(k), rs).start()

            @pl.when(k != 0)
            def _():
                remote(src(k), dst(k), ss, rs, target(k)).start()

    for h in range(2):
        arrived(xin.at[0, :, pl.ds(h * HALF, HALF)], x_s.at[0, h], x_r.at[0, h])

        @pl.loop(0, NC)
        def _(ch):
            select(0, h, ch)
            deliver(
                ch, lambda k: fsend.at[0, k, h], lambda k: frecv.at[0, k, h], f_s.at[0], f_r.at[h * NC + ch], there
            )

        if h == 0:
            exchange(1, 0, scaled)
            exchange(1, 1, scaled)

    load_s.wait()
    pi = lax.broadcasted_iota(I32, (ROWS, ROWS), 0)
    qi = lax.broadcasted_iota(I32, (ROWS, ROWS), 1)
    dy, kk, c3 = row_parts(pi)
    origin = (((z - (kk >> 1)) & 7) * 8 + ((y - dy) & 3) * 2 + (c ^ (kk & 1))) * CAP + c3
    natural = (limit[...] * spike_v[...].astype(F32) / STEPS).astype(BF16)
    ordered = dot(one_hot(qi == origin), natural).astype(BF16)
    for ch in range(NC):
        act[ch, r] = ordered[ch * HOME : (ch + 1) * HOME]

    for h in range(2):
        arrived(xin.at[1, :, pl.ds(h * HALF, HALF)], x_s.at[1, h], x_r.at[1, h])

    @pl.loop(0, NC)
    def _(ch):
        select(1, 0, ch)
        select(1, 1, ch)

    def send_g(ch):
        deliver(ch, lambda k: fsend.at[1, k], lambda k: frecv.at[1, k], f_s.at[1], f_r.at[2 * NC + ch], there)

    load_in.wait()
    load_out.wait()

    def compact(a, ch):
        at = pl.ds(pl.multiple_of(ch * ROWS, ROWS), ROWS)
        for h in range(2):
            block = frecv[a, pl.ds(ch * KC, KC), h].reshape(MROWS, MAIN)
            rows[a, at, h * HALF : h * HALF + MAIN] = dot(p0[...], block).astype(BF16)
            tail = sum(dot(p1[m], block[:, m * PIECE : (m + 1) * PIECE]) for m in range(3))
            rows[a, at, h * HALF + MAIN : (h + 1) * HALF] = tail.astype(BF16)
        return rows[a, at, :]

    @pl.loop(0, NC)
    def _(ch):
        arrived(frecv.at[0, pl.ds(ch * KC, KC), 0], f_s.at[0], f_r.at[ch])

    @pl.loop(0, NC)
    def _(ch):
        arrived(frecv.at[0, pl.ds(ch * KC, KC), 1], f_s.at[0], f_r.at[NC + ch])

        @pl.when(ch % 2 == 1)
        def _():
            send_g(ch // 2)

        msend[ch] = dot(compact(0, ch), win_v[...]).reshape(ND, HOME, FF)
        for d in (2, 1, 3):
            q = replica(d)
            remote(msend.at[ch, q], mrecv.at[ch, d - 1], m_s, m_r.at[ch], (q, e)).start()

    def upstream(ch):
        arrived(frecv.at[1, pl.ds(ch * KC, KC)], f_s.at[1], f_r.at[2 * NC + ch])

        @pl.when(ch < 2)
        def _():
            send_g(ch + 2)

        part = dot(compact(1, ch), wout_v[...]).reshape(ND, HOME, FF)
        uown[ch] = part
        usend[ch] = part.astype(BF16)
        for d in (2, 1, 3):
            q = replica(d)
            remote(usend.at[ch, q], urecv.at[ch, d - 1], u_s, u_r.at[ch], (q, e)).start()

    def hidden(ch):
        arrived(mrecv.at[ch], m_s, m_r.at[ch])
        arrived(urecv.at[ch], u_s, u_r.at[ch])

        @pl.loop(0, 3)
        def _(i):
            at = pl.ds(pl.multiple_of(i * 16, 16), 16)
            membrane = msend[ch, r, at] + mrecv[ch, 0, at] + mrecv[ch, 1, at] + mrecv[ch, 2, at]
            up = uown[ch, r, at]
            for d in range(3):
                up = up + urecv[ch, d, at].astype(F32)
            total = jnp.zeros_like(membrane)
            for step in range(STEPS):
                sig = jax.nn.sigmoid(SHARP * (membrane - (step + 0.5) * limit[...]))
                total = total + SHARP * sig * (1.0 - sig)
            hid[ch, r, at] = (up * total).astype(BF16)

        for d in (2, 1, 3):
            remote(hid.at[ch, r], hid.at[ch, r], h_s, h_r.at[ch], (replica(d), e)).start()

    def slot_grad(ch):
        arrived(hid.at[ch, pl.ds(0, 3)], h_s, h_r.at[ch])
        sg = dot(hid[ch].reshape(ROWS, FF), win_v[...], ((1,), (1,))).astype(BF16)
        for h in range(2):
            main = dot(pt0[...], sg[:, h * HALF : h * HALF + MAIN])
            tail = sg[:, h * HALF + MAIN : (h + 1) * HALF]
            for m in range(3):
                cols = slice(m * PIECE, (m + 1) * PIECE)
                both = main[:, cols] + dot(pt1[m], tail)
                rsend[h, pl.ds(ch * KC, KC), :, cols] = both.astype(BF16).reshape(KC, 16, PIECE)

    def give_back(h, ch):
        deliver(ch, lambda k: rsend.at[h, k], lambda k: rrecv.at[h, k], r_s.at[h], r_r.at[h * NC + ch], back)

    @pl.loop(0, NC)
    def _(ch):
        upstream(ch)

        @pl.when(ch >= 1)
        def _():
            hidden(ch - 1)

        @pl.when(ch >= 2)
        def _():
            slot_grad(ch - 2)
            give_back(0, ch - 2)

    hidden(NC - 1)
    slot_grad(NC - 2)
    give_back(0, NC - 2)

    def weight_grad(a, right, out):
        @pl.loop(0, 4)
        def _(i):
            at = pl.ds(pl.multiple_of(i * 256, 256), 256)
            wg[a, at, :] = dot(rows[a, :, at], right[...].reshape(NC * ROWS, FF), ((0,), (0,))).astype(BF16)

        pltpu.make_async_copy(wg.at[a], out, w_s.at[a]).start()

    for d in (2, 1, 3):
        remote(act.at[:, r], act.at[:, r], a_s, a_r, (replica(d), e)).start()

    give_back(1, 0)
    slot_grad(NC - 1)
    give_back(0, NC - 1)

    def returned(h, ch):
        arrived(rrecv.at[h, pl.ds(ch * KC, KC)], r_s.at[h], r_r.at[h * NC + ch])

    def combine(h):
        block = rrecv[h].reshape(NC * MROWS, MAIN)
        tsend[h, :, 0:MAIN] = dot(sel0[...], block, ((0,), (0,))).astype(BF16)
        tail = sum(dot(sel1[m], block[:, m * PIECE : (m + 1) * PIECE], ((0,), (0,))) for m in range(3))
        tsend[h, :, MAIN:HALF] = tail.astype(BF16)
        place = tok_out.at[:, pl.ds(pl.multiple_of(r * W + h * HALF, HALF), HALF)]

        def part(q):
            return tsend.at[h, pl.ds(pl.multiple_of(q * TOK, TOK), TOK)]

        pltpu.make_async_copy(part(r), place, t_r.at[h]).start()
        for d in (2, 1, 3):
            q = replica(d)
            remote(part(q), place, t_s.at[h], t_r.at[h], (q, e)).start()

    returned(0, 0)
    returned(0, 1)
    give_back(1, 1)
    returned(0, 2)
    give_back(1, 2)
    weight_grad(0, hid, win_out)
    returned(0, 3)
    give_back(1, 3)
    combine(0)
    arrived(act.at[:, pl.ds(0, 3)], a_s, a_r)
    weight_grad(1, act, wout_out)
    for ch in range(NC):
        returned(1, ch)
    combine(1)

    sent(pos_v.at[pl.ds(0, 3)], pos_s, pos_r)
    for a in range(2):
        for h in range(2):
            sent(xin.at[a, pl.ds(0, 3 * TOK), pl.ds(h * HALF, HALF)], x_s.at[a, h], x_r.at[a, h])
        sent(fsend.at[a, pl.ds(1, NE - 1)], f_s.at[a], f_r.at[0])
    sent(msend.at[pl.ds(0, 3)], m_s, m_r.at[0])
    sent(usend.at[pl.ds(0, 3)], u_s, u_r.at[0])
    sent(hid.at[pl.ds(0, 3)], h_s, h_r.at[0])
    sent(act.at[:, pl.ds(0, 3)], a_s, a_r)
    for h in range(2):
        sent(rsend.at[h, pl.ds(1, NE - 1)], r_s.at[h], r_r.at[h * NC])
        sent(tsend.at[h, pl.ds(0, 3 * TOK)], t_s.at[h], t_r.at[h])
    for a, out in enumerate((win_out, wout_out)):
        pltpu.make_async_copy(wg.at[a], out, w_s.at[a]).wait()
    for h in range(2):
        arrived(tok_out.at[:, pl.ds(0, ND * HALF)], t_s.at[h], t_r.at[h])


def on_device(tokens, grad_out, gate_prob, expert_ids, w_in, w_out, threshold, spike_counts):
    vmem = pl.BlockSpec(memory_space=pltpu.VMEM)
    hbm = pl.BlockSpec(memory_space=pl.ANY)
    dma = pltpu.SemaphoreType.DMA
    out = pl.pallas_call(
        kernel,
        name="moe_backward",
        out_shape=(
            jax.ShapeDtypeStruct((TOK, ND * W), BF16),
            jax.ShapeDtypeStruct((W, FF), BF16),
            jax.ShapeDtypeStruct((W, FF), BF16),
        ),
        in_specs=[vmem, vmem, vmem] + [hbm] * 5,
        out_specs=(hbm, hbm, hbm),
        scratch_shapes=[
            pltpu.VMEM((TOK, ND * W), BF16),
            pltpu.VMEM((TOK, ND * W), BF16),
            pltpu.VMEM((ROWS, FF), I32),
            pltpu.VMEM((W, FF), BF16),
            pltpu.VMEM((W, FF), BF16),
            pltpu.VMEM((ND, 8, TOK), I32),
            pltpu.VMEM((2, ND * TOK, W), BF16),
            pltpu.VMEM((NC * MROWS, ND * TOK), BF16),
            pltpu.VMEM((3, NC * MROWS, ND * TOK), BF16),
            pltpu.VMEM((ROWS, MROWS), BF16),
            pltpu.VMEM((3, ROWS, MROWS), BF16),
            pltpu.VMEM((MROWS, ROWS), BF16),
            pltpu.VMEM((3, MROWS, ROWS), BF16),
            pltpu.VMEM((2, NE, 2, 16, MAIN), BF16),
            pltpu.VMEM((2, NE, 2, 16, MAIN), BF16),
            pltpu.VMEM((2, NC * ROWS, W), BF16),
            pltpu.VMEM((NC, ND, HOME, FF), F32),
            pltpu.VMEM((NC, 3, HOME, FF), F32),
            pltpu.VMEM((NC, ND, HOME, FF), F32),
            pltpu.VMEM((NC, ND, HOME, FF), BF16),
            pltpu.VMEM((NC, 3, HOME, FF), BF16),
            pltpu.VMEM((NC, ND, HOME, FF), BF16),
            pltpu.VMEM((NC, ND, HOME, FF), BF16),
            pltpu.VMEM((2, NE, 16, MAIN), BF16),
            pltpu.VMEM((2, NE, 16, MAIN), BF16),
            pltpu.VMEM((2, ND * TOK, HALF), BF16),
            pltpu.VMEM((2, W, FF), BF16),
            dma((4,)),
            dma, dma,
            dma((2, 2)), dma((2, 2)),
            dma((2,)), dma((3 * NC,)),
            dma, dma((NC,)),
            dma, dma((NC,)),
            dma, dma((NC,)),
            dma, dma,
            dma((2,)), dma((2 * NC,)),
            dma((2,)), dma((2,)),
            dma((2,)),
        ],
        compiler_params=pltpu.CompilerParams(
            collective_id=0, has_side_effects=True, vmem_limit_bytes=58 << 20
        ),
        cost_estimate=pl.CostEstimate(flops=9 * 10**9, bytes_accessed=14 << 20, transcendentals=1 << 20),
    )(
        gate_prob.reshape(1, TOK), expert_ids.reshape(1, TOK), threshold, tokens, grad_out,
        w_in.reshape(W, FF), w_out.reshape(W, FF), spike_counts.reshape(ROWS, FF),
    )
    return out[0], out[1][None], out[2][None]


def solution(mesh):
    placed = (
        P(("dp", "expert"), None),
        P(("dp", "expert"), None),
        P(("dp", "expert")),
        P(("dp", "expert"), None),
        P("expert", "dp", None),
        P("expert", "dp", None),
        P("expert", None),
        P("expert", "dp", None),
    )
    return jax.shard_map(
        on_device,
        mesh=mesh,
        in_specs=placed,
        out_specs=(P(("dp", "expert"), None), P("expert", "dp", None), P("expert", "dp", None)),
        check_vma=False,
    )
```

```python
import functools
import jax
import jax.numpy as jnp
from jax import lax
from jax.experimental import pallas as pl
from jax.experimental.pallas import tpu as pltpu
from jax.sharding import PartitionSpec as P

STEPS = 4
SHARP = 4.0
TOK = 128
CAP = 3
NE = 64
ND = 4
W = 1024
FF = 1024
HALF = 512
MAIN = 384
PIECE = 128
NC = 4
KC = 16
ROWS = 192
HOME = 48
MROWS = KC * 16
F32, BF16, I32 = jnp.float32, jnp.bfloat16, jnp.int32
MESH = pl.DeviceIdType.MESH


def dot(a, b, dims=((1,), (0,))):
    return lax.dot_general(a, b, (dims, ((), ())), preferred_element_type=F32)


def one_hot(cond):
    return jnp.where(cond, 1.0, 0.0).astype(BF16)


def row_parts(p):
    rr = (p >= 48).astype(I32) + (p >= 96).astype(I32) + (p >= 144).astype(I32)
    pp = p - 48 * rr
    kk = (pp * 171) >> 9
    return rr, kk, pp - 3 * kk


def spread(p, q, m):
    rr, kk, c3 = row_parts(p)
    rho = rr * 3 + c3
    if m is None:
        return q == kk * 16 + rho
    return (q == kk * 16 + 12 + (rho & 3)) & ((rho >> 2) == m)


def kernel(
    gate, ids, limit, tokens, grads, w_in, w_out, spikes,
    tok_out, win_out, wout_out,
    grad_v, scaled, spike_v, win_v, wout_v, pos_v, xin, sel0, sel1, p0, p1, pt0, pt1,
    fsend, frecv, rows, msend, mfwd, mrecv, uown, usend, urecv, hid, act, rsend, rrecv, tsend,
    lsem, pos_s, pos_r, x_s, x_r, f_s, f_r, fw_s, fw_r, m_s, m_r, u_s, u_r, h_s, h_r, a_s, a_r, r_s, r_r, t_s, t_r,
):
    r = lax.axis_index("dp")
    e = lax.axis_index("expert")
    z, y, c = e // 8, (e // 2) % 4, e % 2

    def there(k):
        dy, dz, dc = k // 16, (k // 2) % 8, k % 2
        return (r, ((z + dz) % 8) * 8 + ((y + dy) % 4) * 2 + (c + dc) % 2)

    def back(k):
        dy, dz, dc = k // 16, (k // 2) % 8, k % 2
        return (r, ((z + 8 - dz) % 8) * 8 + ((y + 4 - dy) % 4) * 2 + (c + dc) % 2)

    def replica(d):
        return (r + d) % ND

    def remote(src, dst, ss, rs, device):
        return pltpu.make_async_remote_copy(
            src_ref=src, dst_ref=dst, send_sem=ss, recv_sem=rs, device_id=device, device_id_type=MESH
        )

    def arrived(ref, ss, rs):
        remote(ref, ref, ss, rs, (replica(1), e)).wait_recv()

    def sent(ref, ss, rs):
        remote(ref, ref, ss, rs, (replica(1), e)).wait_send()

    def order(i):
        dzi = i // 2
        half = dzi // 2
        return (half + (dzi % 2) * (7 - 2 * half)) * 2 + i % 2

    load_g = pltpu.make_async_copy(grads, grad_v, lsem.at[0])
    load_g.start()
    load_in = pltpu.make_async_copy(w_in, win_v, lsem.at[1])
    load_in.start()
    load_out = pltpu.make_async_copy(w_out, wout_v, lsem.at[2])
    load_out.start()
    load_s = pltpu.make_async_copy(spikes, spike_v, lsem.at[3])
    load_s.start()

    barrier = pltpu.get_barrier_semaphore()

    @pl.loop(1, NE)
    def _(k):
        pl.semaphore_signal(barrier, inc=1, device_id=there(k), device_id_type=MESH)

    for d in range(1, ND):
        pl.semaphore_signal(barrier, inc=1, device_id=(replica(d), e), device_id_type=MESH)

    row = ids[...]
    ti = lax.broadcasted_iota(I32, (TOK, TOK), 0)
    tj = lax.broadcasted_iota(I32, (TOK, TOK), 1)
    col = jnp.sum(jnp.where(ti == tj, row, 0), axis=1, keepdims=True)
    slot = jnp.sum(jnp.where((col == row) & (ti < tj), 1, 0), axis=0, keepdims=True)
    kidx = ((((row >> 1) & 3) - y) & 3) * 16 + (((row >> 3) - z) & 7) * 2 + ((row & 1) ^ c)
    pos = kidx * 16 + r * CAP + slot
    pos_v[r] = jnp.broadcast_to(pos, (8, TOK))

    pl.semaphore_wait(barrier, NE - 1 + ND - 1)

    for d in (2, 1, 3):
        remote(pos_v.at[r], pos_v.at[r], pos_s, pos_r, (replica(d), e)).start()

    def exchange(a, h, source):
        mine = xin.at[a, pl.ds(pl.multiple_of(r * TOK, TOK), TOK), pl.ds(h * HALF, HALF)]

        def piece(q):
            return source.at[:, pl.ds(pl.multiple_of(q * W + h * HALF, HALF), HALF)]

        pltpu.make_async_copy(piece(r), mine, x_r.at[a, h]).start()
        for d in (2, 1, 3):
            remote(piece(replica(d)), mine, x_s.at[a, h], x_r.at[a, h], (replica(d), e)).start()

    exchange(0, 0, tokens)

    load_g.wait()
    gate_col = jnp.sum(jnp.where(ti == tj, gate[...], 0.0), axis=1, keepdims=True)

    @pl.loop(0, 8)
    def _(i):
        cols = pl.ds(pl.multiple_of(i * 512, 512), 512)
        scaled[:, cols] = (gate_col * grad_v[:, cols].astype(F32)).astype(BF16)

    exchange(0, 1, tokens)

    pi = lax.broadcasted_iota(I32, (ROWS, MROWS), 0)
    qi = lax.broadcasted_iota(I32, (ROWS, MROWS), 1)
    p0[...] = one_hot(spread(pi, qi, None))
    for m in range(3):
        p1[m] = one_hot(spread(pi, qi, m))
    pi = lax.broadcasted_iota(I32, (MROWS, ROWS), 1)
    qi = lax.broadcasted_iota(I32, (MROWS, ROWS), 0)
    pt0[...] = one_hot(spread(pi, qi, None))
    for m in range(3):
        pt1[m] = one_hot(spread(pi, qi, m))

    arrived(pos_v.at[pl.ds(0, 3)], pos_s, pos_r)

    @pl.loop(0, NC)
    def _(ch):
        base = ch * MROWS
        qi = lax.broadcasted_iota(I32, (MROWS, TOK), 0) + base
        at = pl.ds(pl.multiple_of(base, MROWS), MROWS)
        for q in range(ND):
            where = pos_v[q][0:1]
            rho = where & 15
            tail = where - rho + 12 + (rho & 3)
            cols = slice(q * TOK, (q + 1) * TOK)
            sel0[at, cols] = one_hot(qi == where)
            for m in range(3):
                sel1[m, at, cols] = one_hot(qi == jnp.where((rho >> 2) == m, tail, -1))

    def select(a, h, ch):
        at = pl.ds(pl.multiple_of(ch * MROWS, MROWS), MROWS)
        main = dot(sel0[at, :], xin[a, :, h * HALF : h * HALF + MAIN])
        tail = xin[a, :, h * HALF + MAIN : (h + 1) * HALF]
        for m in range(3):
            cols = slice(m * PIECE, (m + 1) * PIECE)
            both = main[:, cols] + dot(sel1[m, at, :], tail)
            fsend[a, pl.ds(ch * KC, KC), h, :, cols] = both.astype(BF16).reshape(KC, 16, PIECE)

    def deliver(ch, src, dst, ss, rs, target):
        @pl.loop(0, KC)
        def _(i):
            k = ch * KC + order(i)

            @pl.when(k == 0)
            def _():
                pltpu.make_async_copy(src(k), dst(k), rs).start()

            @pl.when(k != 0)
            def _():
                remote(src(k), dst(k), ss, rs, target(k)).start()

    for h in range(2):
        arrived(xin.at[0, :, pl.ds(h * HALF, HALF)], x_s.at[0, h], x_r.at[0, h])

        @pl.loop(0, NC)
        def _(ch):
            select(0, h, ch)
            deliver(
                ch, lambda k: fsend.at[0, k, h], lambda k: frecv.at[0, k, h], f_s.at[0], f_r.at[h * NC + ch], there
            )

        if h == 0:
            exchange(1, 0, scaled)
            exchange(1, 1, scaled)

    load_s.wait()
    pi = lax.broadcasted_iota(I32, (ROWS, ROWS), 0)
    qi = lax.broadcasted_iota(I32, (ROWS, ROWS), 1)
    dy, kk, c3 = row_parts(pi)
    origin = (((z - (kk >> 1)) & 7) * 8 + ((y - dy) & 3) * 2 + (c ^ (kk & 1))) * CAP + c3
    natural = (limit[...] * spike_v[...].astype(F32) / STEPS).astype(BF16)
    ordered = dot(one_hot(qi == origin), natural).astype(BF16)
    for ch in range(NC):
        act[ch, r] = ordered[ch * HOME : (ch + 1) * HOME]

    for h in range(2):
        arrived(xin.at[1, :, pl.ds(h * HALF, HALF)], x_s.at[1, h], x_r.at[1, h])

    @pl.loop(0, NC)
    def _(ch):
        select(1, 0, ch)
        select(1, 1, ch)

    def send_g(ch):
        deliver(ch, lambda k: fsend.at[1, k], lambda k: frecv.at[1, k], f_s.at[1], f_r.at[2 * NC + ch], there)

    load_in.wait()
    load_out.wait()

    def relay(ch):
        arrived(mfwd.at[ch], fw_s, fw_r.at[ch])
        for i, d in enumerate((1, 3)):
            q = replica(d)
            at = pl.ds(i * 24, 24)
            msend[ch, q, at] = msend[ch, q, at] + mfwd[ch, i]
            remote(msend.at[ch, q], mrecv.at[ch, i], m_s, m_r.at[ch], (q, e)).start()

    def compact(a, ch):
        at = pl.ds(pl.multiple_of(ch * ROWS, ROWS), ROWS)
        for h in range(2):
            block = frecv[a, pl.ds(ch * KC, KC), h].reshape(MROWS, MAIN)
            rows[a, at, h * HALF : h * HALF + MAIN] = dot(p0[...], block).astype(BF16)
            tail = sum(dot(p1[m], block[:, m * PIECE : (m + 1) * PIECE]) for m in range(3))
            rows[a, at, h * HALF + MAIN : (h + 1) * HALF] = tail.astype(BF16)
        return rows[a, at, :]

    @pl.loop(0, NC)
    def _(ch):
        arrived(frecv.at[0, pl.ds(ch * KC, KC), 0], f_s.at[0], f_r.at[ch])

    @pl.loop(0, NC)
    def _(ch):
        arrived(frecv.at[0, pl.ds(ch * KC, KC), 1], f_s.at[0], f_r.at[NC + ch])

        @pl.when(ch % 2 == 1)
        def _():
            send_g(ch // 2)

        msend[ch] = dot(compact(0, ch), win_v[...]).reshape(ND, HOME, FF)
        far = replica(2)
        for i, d in enumerate((1, 3)):
            part = msend.at[ch, far, pl.ds(i * 24, 24)]
            remote(part, mfwd.at[ch, i], fw_s, fw_r.at[ch], (replica(d), e)).start()

        @pl.when(ch >= 1)
        def _():
            relay(ch - 1)

    relay(NC - 1)

    def upstream(ch):
        arrived(frecv.at[1, pl.ds(ch * KC, KC)], f_s.at[1], f_r.at[2 * NC + ch])

        @pl.when(ch < 2)
        def _():
            send_g(ch + 2)

        part = dot(compact(1, ch), wout_v[...]).reshape(ND, HOME, FF)
        uown[ch] = part
        usend[ch] = part.astype(BF16)
        for d in (2, 1, 3):
            q = replica(d)
            remote(usend.at[ch, q], urecv.at[ch, d - 1], u_s, u_r.at[ch], (q, e)).start()

    def hidden(ch):
        arrived(mrecv.at[ch], m_s, m_r.at[ch])
        arrived(urecv.at[ch], u_s, u_r.at[ch])

        @pl.loop(0, 3)
        def _(i):
            at = pl.ds(pl.multiple_of(i * 16, 16), 16)
            membrane = msend[ch, r, at] + mrecv[ch, 0, at] + mrecv[ch, 1, at]
            up = uown[ch, r, at]
            for d in range(3):
                up = up + urecv[ch, d, at].astype(F32)
            total = jnp.zeros_like(membrane)
            for step in range(STEPS):
                sig = jax.nn.sigmoid(SHARP * (membrane - (step + 0.5) * limit[...]))
                total = total + SHARP * sig * (1.0 - sig)
            hid[ch, r, at] = (up * total).astype(BF16)

        for d in (2, 1, 3):
            remote(hid.at[ch, r], hid.at[ch, r], h_s, h_r.at[ch], (replica(d), e)).start()

    def slot_grad(ch):
        arrived(hid.at[ch, pl.ds(0, 3)], h_s, h_r.at[ch])
        sg = dot(hid[ch].reshape(ROWS, FF), win_v[...], ((1,), (1,))).astype(BF16)
        for h in range(2):
            main = dot(pt0[...], sg[:, h * HALF : h * HALF + MAIN])
            tail = sg[:, h * HALF + MAIN : (h + 1) * HALF]
            for m in range(3):
                cols = slice(m * PIECE, (m + 1) * PIECE)
                both = main[:, cols] + dot(pt1[m], tail)
                rsend[h, pl.ds(ch * KC, KC), :, cols] = both.astype(BF16).reshape(KC, 16, PIECE)

    def give_back(h, ch):
        deliver(ch, lambda k: rsend.at[h, k], lambda k: rrecv.at[h, k], r_s.at[h], r_r.at[h * NC + ch], back)

    @pl.loop(0, NC)
    def _(ch):
        upstream(ch)

        @pl.when(ch >= 1)
        def _():
            hidden(ch - 1)

        @pl.when(ch >= 2)
        def _():
            slot_grad(ch - 2)
            give_back(0, ch - 2)

    hidden(NC - 1)
    slot_grad(NC - 2)
    give_back(0, NC - 2)

    def weight_grad(a, right, out):
        @pl.loop(0, 4)
        def _(i):
            at = pl.ds(pl.multiple_of(i * 256, 256), 256)
            out[at, :] = dot(rows[a, :, at], right[...].reshape(NC * ROWS, FF), ((0,), (0,))).astype(BF16)


    for d in (2, 1, 3):
        remote(act.at[:, r], act.at[:, r], a_s, a_r, (replica(d), e)).start()

    give_back(1, 0)
    slot_grad(NC - 1)
    give_back(0, NC - 1)

    def returned(h, ch):
        arrived(rrecv.at[h, pl.ds(ch * KC, KC)], r_s.at[h], r_r.at[h * NC + ch])

    def combine(h):
        block = rrecv[h].reshape(NC * MROWS, MAIN)
        tsend[h, :, 0:MAIN] = dot(sel0[...], block, ((0,), (0,))).astype(BF16)
        tail = sum(dot(sel1[m], block[:, m * PIECE : (m + 1) * PIECE], ((0,), (0,))) for m in range(3))
        tsend[h, :, MAIN:HALF] = tail.astype(BF16)
        place = tok_out.at[:, pl.ds(pl.multiple_of(r * W + h * HALF, HALF), HALF)]

        def part(q):
            return tsend.at[h, pl.ds(pl.multiple_of(q * TOK, TOK), TOK)]

        pltpu.make_async_copy(part(r), place, t_r.at[h]).start()
        for d in (2, 1, 3):
            q = replica(d)
            remote(part(q), place, t_s.at[h], t_r.at[h], (q, e)).start()

    returned(0, 0)
    returned(0, 1)
    give_back(1, 1)
    returned(0, 2)
    give_back(1, 2)
    weight_grad(0, hid, win_out)
    returned(0, 3)
    give_back(1, 3)
    combine(0)
    arrived(act.at[:, pl.ds(0, 3)], a_s, a_r)
    weight_grad(1, act, wout_out)
    for ch in range(NC):
        returned(1, ch)
    combine(1)

    sent(pos_v.at[pl.ds(0, 3)], pos_s, pos_r)
    for a in range(2):
        for h in range(2):
            sent(xin.at[a, pl.ds(0, 3 * TOK), pl.ds(h * HALF, HALF)], x_s.at[a, h], x_r.at[a, h])
        sent(fsend.at[a, pl.ds(1, NE - 1)], f_s.at[a], f_r.at[0])
    sent(msend.at[pl.ds(0, 2)], m_s, m_r.at[0])
    sent(msend.at[0], fw_s, fw_r.at[0])
    sent(usend.at[pl.ds(0, 3)], u_s, u_r.at[0])
    sent(hid.at[pl.ds(0, 3)], h_s, h_r.at[0])
    sent(act.at[:, pl.ds(0, 3)], a_s, a_r)
    for h in range(2):
        sent(rsend.at[h, pl.ds(1, NE - 1)], r_s.at[h], r_r.at[h * NC])
        sent(tsend.at[h, pl.ds(0, 3 * TOK)], t_s.at[h], t_r.at[h])
    for h in range(2):
        arrived(tok_out.at[:, pl.ds(0, ND * HALF)], t_s.at[h], t_r.at[h])


def on_device(tokens, grad_out, gate_prob, expert_ids, w_in, w_out, threshold, spike_counts):
    vmem = pl.BlockSpec(memory_space=pltpu.VMEM)
    hbm = pl.BlockSpec(memory_space=pl.ANY)
    dma = pltpu.SemaphoreType.DMA
    out = pl.pallas_call(
        kernel,
        name="moe_backward",
        out_shape=(
            pltpu.VMEM((TOK, ND * W), BF16),
            pltpu.VMEM((W, FF), BF16),
            pltpu.VMEM((W, FF), BF16),
        ),
        in_specs=[vmem, vmem, vmem] + [hbm] * 5,
        out_specs=(vmem, vmem, vmem),
        scratch_shapes=[
            pltpu.VMEM((TOK, ND * W), BF16),
            pltpu.VMEM((TOK, ND * W), BF16),
            pltpu.VMEM((ROWS, FF), I32),
            pltpu.VMEM((W, FF), BF16),
            pltpu.VMEM((W, FF), BF16),
            pltpu.VMEM((ND, 8, TOK), I32),
            pltpu.VMEM((2, ND * TOK, W), BF16),
            pltpu.VMEM((NC * MROWS, ND * TOK), BF16),
            pltpu.VMEM((3, NC * MROWS, ND * TOK), BF16),
            pltpu.VMEM((ROWS, MROWS), BF16),
            pltpu.VMEM((3, ROWS, MROWS), BF16),
            pltpu.VMEM((MROWS, ROWS), BF16),
            pltpu.VMEM((3, MROWS, ROWS), BF16),
            pltpu.VMEM((2, NE, 2, 16, MAIN), BF16),
            pltpu.VMEM((2, NE, 2, 16, MAIN), BF16),
            pltpu.VMEM((2, NC * ROWS, W), BF16),
            pltpu.VMEM((NC, ND, HOME, FF), F32),
            pltpu.VMEM((NC, 2, 24, FF), F32),
            pltpu.VMEM((NC, 2, HOME, FF), F32),
            pltpu.VMEM((NC, ND, HOME, FF), F32),
            pltpu.VMEM((NC, ND, HOME, FF), BF16),
            pltpu.VMEM((NC, 3, HOME, FF), BF16),
            pltpu.VMEM((NC, ND, HOME, FF), BF16),
            pltpu.VMEM((NC, ND, HOME, FF), BF16),
            pltpu.VMEM((2, NE, 16, MAIN), BF16),
            pltpu.VMEM((2, NE, 16, MAIN), BF16),
            pltpu.VMEM((2, ND * TOK, HALF), BF16),
            dma((4,)),
            dma, dma,
            dma((2, 2)), dma((2, 2)),
            dma((2,)), dma((3 * NC,)),
            dma, dma((NC,)),
            dma, dma((NC,)),
            dma, dma((NC,)),
            dma, dma((NC,)),
            dma, dma,
            dma((2,)), dma((2 * NC,)),
            dma((2,)), dma((2,)),
        ],
        compiler_params=pltpu.CompilerParams(
            collective_id=0, has_side_effects=True, vmem_limit_bytes=52 << 20
        ),
        cost_estimate=pl.CostEstimate(flops=9 * 10**9, bytes_accessed=14 << 20, transcendentals=1 << 20),
    )(
        gate_prob.reshape(1, TOK), expert_ids.reshape(1, TOK), threshold, tokens, grad_out,
        w_in.reshape(W, FF), w_out.reshape(W, FF), spike_counts.reshape(ROWS, FF),
    )
    return out[0], out[1][None], out[2][None]


def solution(mesh):
    placed = (
        P(("dp", "expert"), None),
        P(("dp", "expert"), None),
        P(("dp", "expert")),
        P(("dp", "expert"), None),
        P("expert", "dp", None),
        P("expert", "dp", None),
        P("expert", None),
        P("expert", "dp", None),
    )
    return jax.shard_map(
        on_device,
        mesh=mesh,
        in_specs=placed,
        out_specs=(P(("dp", "expert"), None), P("expert", "dp", None), P("expert", "dp", None)),
        check_vma=False,
    )
```

```python
import functools
import jax
import jax.numpy as jnp
from jax import lax
from jax.experimental import pallas as pl
from jax.experimental.pallas import tpu as pltpu
from jax.sharding import PartitionSpec as P

STEPS = 4
SHARP = 4.0
TOK = 128
CAP = 3
NE = 64
ND = 4
W = 1024
FF = 1024
HALF = 512
MAIN = 384
PIECE = 128
NC = 4
KC = 16
ROWS = 192
HOME = 48
MROWS = KC * 16
F32, BF16, I32 = jnp.float32, jnp.bfloat16, jnp.int32
MESH = pl.DeviceIdType.MESH


def dot(a, b, dims=((1,), (0,))):
    return lax.dot_general(a, b, (dims, ((), ())), preferred_element_type=F32)


def one_hot(cond):
    return jnp.where(cond, 1.0, 0.0).astype(BF16)


def row_parts(p):
    rr = (p >= 48).astype(I32) + (p >= 96).astype(I32) + (p >= 144).astype(I32)
    pp = p - 48 * rr
    kk = (pp * 171) >> 9
    return rr, kk, pp - 3 * kk


def spread(p, q, m):
    rr, kk, c3 = row_parts(p)
    rho = rr * 3 + c3
    if m is None:
        return q == kk * 16 + rho
    return (q == kk * 16 + 12 + (rho & 3)) & ((rho >> 2) == m)


def kernel(
    gate, ids, limit, tokens, grads, w_in, w_out, spikes,
    tok_out, win_out, wout_out,
    grad_v, scaled, spike_v, win_v, wout_v, pos_v, xin, sel0, sel1, p0, p1, pt0, pt1,
    fsend, frecv, rows, msend, mfwd, mrecv, uown, usend, urecv, hid, act, rsend, rrecv, tsend,
    lsem, pos_s, pos_r, x_s, x_r, f_s, f_r, fw_s, fw_r, m_s, m_r, u_s, u_r, h_s, h_r, a_s, a_r, r_s, r_r, t_s, t_r,
):
    r = lax.axis_index("dp")
    e = lax.axis_index("expert")
    z, y, c = e // 8, (e // 2) % 4, e % 2

    def there(k):
        dy, dz, dc = k // 16, (k // 2) % 8, k % 2
        return (r, ((z + dz) % 8) * 8 + ((y + dy) % 4) * 2 + (c + dc) % 2)

    def back(k):
        dy, dz, dc = k // 16, (k // 2) % 8, k % 2
        return (r, ((z + 8 - dz) % 8) * 8 + ((y + 4 - dy) % 4) * 2 + (c + dc) % 2)

    def replica(d):
        return (r + d) % ND

    def remote(src, dst, ss, rs, device):
        return pltpu.make_async_remote_copy(
            src_ref=src, dst_ref=dst, send_sem=ss, recv_sem=rs, device_id=device, device_id_type=MESH
        )

    def arrived(ref, ss, rs):
        remote(ref, ref, ss, rs, (replica(1), e)).wait_recv()

    def sent(ref, ss, rs):
        remote(ref, ref, ss, rs, (replica(1), e)).wait_send()

    def order(i):
        dzi = i // 2
        half = dzi // 2
        return (half + (dzi % 2) * (7 - 2 * half)) * 2 + i % 2

    load_g = pltpu.make_async_copy(grads, grad_v, lsem.at[0])
    load_g.start()
    load_in = pltpu.make_async_copy(w_in, win_v, lsem.at[1])
    load_in.start()
    load_out = pltpu.make_async_copy(w_out, wout_v, lsem.at[2])
    load_out.start()
    load_s = pltpu.make_async_copy(spikes, spike_v, lsem.at[3])
    load_s.start()

    barrier = pltpu.get_barrier_semaphore()

    @pl.loop(1, NE)
    def _(k):
        pl.semaphore_signal(barrier, inc=1, device_id=there(k), device_id_type=MESH)

    for d in range(1, ND):
        pl.semaphore_signal(barrier, inc=1, device_id=(replica(d), e), device_id_type=MESH)

    row = ids[...]
    ti = lax.broadcasted_iota(I32, (TOK, TOK), 0)
    tj = lax.broadcasted_iota(I32, (TOK, TOK), 1)
    col = jnp.sum(jnp.where(ti == tj, row, 0), axis=1, keepdims=True)
    slot = jnp.sum(jnp.where((col == row) & (ti < tj), 1, 0), axis=0, keepdims=True)
    kidx = ((((row >> 1) & 3) - y) & 3) * 16 + (((row >> 3) - z) & 7) * 2 + ((row & 1) ^ c)
    pos = kidx * 16 + r * CAP + slot
    pos_v[r] = jnp.broadcast_to(pos, (8, TOK))

    pl.semaphore_wait(barrier, NE - 1 + ND - 1)

    for d in (2, 1, 3):
        remote(pos_v.at[r], pos_v.at[r], pos_s, pos_r, (replica(d), e)).start()

    def exchange(a, h, source):
        mine = xin.at[a, pl.ds(pl.multiple_of(r * TOK, TOK), TOK), pl.ds(h * HALF, HALF)]

        def piece(q):
            return source.at[:, pl.ds(pl.multiple_of(q * W + h * HALF, HALF), HALF)]

        pltpu.make_async_copy(piece(r), mine, x_r.at[a, h]).start()
        for d in (2, 1, 3):
            remote(piece(replica(d)), mine, x_s.at[a, h], x_r.at[a, h], (replica(d), e)).start()

    exchange(0, 0, tokens)

    load_g.wait()
    gate_col = jnp.sum(jnp.where(ti == tj, gate[...], 0.0), axis=1, keepdims=True)

    @pl.loop(0, 8)
    def _(i):
        cols = pl.ds(pl.multiple_of(i * 512, 512), 512)
        scaled[:, cols] = (gate_col * grad_v[:, cols].astype(F32)).astype(BF16)

    exchange(0, 1, tokens)

    pi = lax.broadcasted_iota(I32, (ROWS, MROWS), 0)
    qi = lax.broadcasted_iota(I32, (ROWS, MROWS), 1)
    p0[...] = one_hot(spread(pi, qi, None))
    for m in range(3):
        p1[m] = one_hot(spread(pi, qi, m))
    pi = lax.broadcasted_iota(I32, (MROWS, ROWS), 1)
    qi = lax.broadcasted_iota(I32, (MROWS, ROWS), 0)
    pt0[...] = one_hot(spread(pi, qi, None))
    for m in range(3):
        pt1[m] = one_hot(spread(pi, qi, m))

    arrived(pos_v.at[pl.ds(0, 3)], pos_s, pos_r)

    @pl.loop(0, NC)
    def _(ch):
        base = ch * MROWS
        qi = lax.broadcasted_iota(I32, (MROWS, TOK), 0) + base
        at = pl.ds(pl.multiple_of(base, MROWS), MROWS)
        for q in range(ND):
            where = pos_v[q][0:1]
            rho = where & 15
            tail = where - rho + 12 + (rho & 3)
            cols = slice(q * TOK, (q + 1) * TOK)
            sel0[at, cols] = one_hot(qi == where)
            for m in range(3):
                sel1[m, at, cols] = one_hot(qi == jnp.where((rho >> 2) == m, tail, -1))

    def select(a, h, ch):
        at = pl.ds(pl.multiple_of(ch * MROWS, MROWS), MROWS)
        main = dot(sel0[at, :], xin[a, :, h * HALF : h * HALF + MAIN])
        tail = xin[a, :, h * HALF + MAIN : (h + 1) * HALF]
        for m in range(3):
            cols = slice(m * PIECE, (m + 1) * PIECE)
            both = main[:, cols] + dot(sel1[m, at, :], tail)
            fsend[a, pl.ds(ch * KC, KC), h, :, cols] = both.astype(BF16).reshape(KC, 16, PIECE)

    def deliver(ch, src, dst, ss, rs, target):
        @pl.loop(0, KC)
        def _(i):
            k = ch * KC + order(i)

            @pl.when(k == 0)
            def _():
                pltpu.make_async_copy(src(k), dst(k), rs).start()

            @pl.when(k != 0)
            def _():
                remote(src(k), dst(k), ss, rs, target(k)).start()

    for h in range(2):
        arrived(xin.at[0, :, pl.ds(h * HALF, HALF)], x_s.at[0, h], x_r.at[0, h])

        @pl.loop(0, NC)
        def _(ch):
            select(0, h, ch)
            deliver(
                ch, lambda k: fsend.at[0, k, h], lambda k: frecv.at[0, k, h], f_s.at[0], f_r.at[h * NC + ch], there
            )

        if h == 0:
            exchange(1, 0, scaled)
            exchange(1, 1, scaled)

    load_s.wait()
    pi = lax.broadcasted_iota(I32, (ROWS, ROWS), 0)
    qi = lax.broadcasted_iota(I32, (ROWS, ROWS), 1)
    dy, kk, c3 = row_parts(pi)
    origin = (((z - (kk >> 1)) & 7) * 8 + ((y - dy) & 3) * 2 + (c ^ (kk & 1))) * CAP + c3
    natural = (limit[...] * spike_v[...].astype(F32) / STEPS).astype(BF16)
    ordered = dot(one_hot(qi == origin), natural).astype(BF16)
    for ch in range(NC):
        act[ch, r] = ordered[ch * HOME : (ch + 1) * HOME]

    for h in range(2):
        arrived(xin.at[1, :, pl.ds(h * HALF, HALF)], x_s.at[1, h], x_r.at[1, h])

    @pl.loop(0, NC)
    def _(ch):
        select(1, 0, ch)
        select(1, 1, ch)

    def send_g(ch):
        deliver(ch, lambda k: fsend.at[1, k], lambda k: frecv.at[1, k], f_s.at[1], f_r.at[2 * NC + ch], there)

    load_in.wait()
    load_out.wait()

    def relay(ch):
        arrived(mfwd.at[ch], fw_s, fw_r.at[ch])
        for i, d in enumerate((1, 3)):
            q = replica(d)
            at = pl.ds(i * 24, 24)
            msend[ch, q, at] = msend[ch, q, at] + mfwd[ch, i]
            remote(msend.at[ch, q], mrecv.at[ch, i], m_s, m_r.at[ch], (q, e)).start()

    def compact(a, ch):
        at = pl.ds(pl.multiple_of(ch * ROWS, ROWS), ROWS)
        for h in range(2):
            block = frecv[a, pl.ds(ch * KC, KC), h].reshape(MROWS, MAIN)
            rows[a, at, h * HALF : h * HALF + MAIN] = dot(p0[...], block).astype(BF16)
            tail = sum(dot(p1[m], block[:, m * PIECE : (m + 1) * PIECE]) for m in range(3))
            rows[a, at, h * HALF + MAIN : (h + 1) * HALF] = tail.astype(BF16)
        return rows[a, at, :]

    @pl.loop(0, NC)
    def _(ch):
        arrived(frecv.at[0, pl.ds(ch * KC, KC), 0], f_s.at[0], f_r.at[ch])

    @pl.loop(0, NC)
    def _(ch):
        arrived(frecv.at[0, pl.ds(ch * KC, KC), 1], f_s.at[0], f_r.at[NC + ch])

        @pl.when(ch % 2 == 1)
        def _():
            send_g(ch // 2)

        msend[ch] = dot(compact(0, ch), win_v[...]).reshape(ND, HOME, FF)
        far = replica(2)
        for i, d in enumerate((1, 3)):
            part = msend.at[ch, far, pl.ds(i * 24, 24)]
            remote(part, mfwd.at[ch, i], fw_s, fw_r.at[ch], (replica(d), e)).start()

        @pl.when(ch >= 1)
        def _():
            relay(ch - 1)

    relay(NC - 1)

    def upstream(ch):
        arrived(frecv.at[1, pl.ds(ch * KC, KC)], f_s.at[1], f_r.at[2 * NC + ch])

        @pl.when(ch < 2)
        def _():
            send_g(ch + 2)

        part = dot(compact(1, ch), wout_v[...]).reshape(ND, HOME, FF)
        uown[ch] = part
        usend[ch] = part.astype(BF16)
        for d in (2, 1, 3):
            q = replica(d)
            remote(usend.at[ch, q], urecv.at[ch, d - 1], u_s, u_r.at[ch], (q, e)).start()

    def hidden(ch):
        arrived(mrecv.at[ch], m_s, m_r.at[ch])
        arrived(urecv.at[ch], u_s, u_r.at[ch])

        @pl.loop(0, 3)
        def _(i):
            at = pl.ds(pl.multiple_of(i * 16, 16), 16)
            membrane = msend[ch, r, at] + mrecv[ch, 0, at] + mrecv[ch, 1, at]
            up = uown[ch, r, at]
            for d in range(3):
                up = up + urecv[ch, d, at].astype(F32)
            total = jnp.zeros_like(membrane)
            for step in range(STEPS):
                sig = jax.nn.sigmoid(SHARP * (membrane - (step + 0.5) * limit[...]))
                total = total + SHARP * sig * (1.0 - sig)
            hid[ch, r, at] = (up * total).astype(BF16)

        for d in (2, 1, 3):
            remote(hid.at[ch, r], hid.at[ch, r], h_s, h_r.at[ch], (replica(d), e)).start()

    def slot_grad(ch):
        arrived(hid.at[ch, pl.ds(0, 3)], h_s, h_r.at[ch])
        sg = dot(hid[ch].reshape(ROWS, FF), win_v[...], ((1,), (1,))).astype(BF16)
        for h in range(2):
            main = dot(pt0[...], sg[:, h * HALF : h * HALF + MAIN])
            tail = sg[:, h * HALF + MAIN : (h + 1) * HALF]
            for m in range(3):
                cols = slice(m * PIECE, (m + 1) * PIECE)
                both = main[:, cols] + dot(pt1[m], tail)
                rsend[h, pl.ds(ch * KC, KC), :, cols] = both.astype(BF16).reshape(KC, 16, PIECE)

    def give_back(h, ch):
        deliver(ch, lambda k: rsend.at[h, k], lambda k: rrecv.at[h, k], r_s.at[h], r_r.at[h * NC + ch], back)

    @pl.loop(0, NC)
    def _(ch):
        upstream(ch)

        @pl.when(ch >= 1)
        def _():
            hidden(ch - 1)

        @pl.when(ch >= 2)
        def _():
            slot_grad(ch - 2)
            give_back(0, ch - 2)

    hidden(NC - 1)
    slot_grad(NC - 2)
    give_back(0, NC - 2)

    def weight_grad(a, right, out):
        @pl.loop(0, 4)
        def _(i):
            at = pl.ds(pl.multiple_of(i * 256, 256), 256)
            out[at, :] = dot(rows[a, :, at], right[...].reshape(NC * ROWS, FF), ((0,), (0,))).astype(BF16)


    give_back(1, 0)
    slot_grad(NC - 1)
    give_back(0, NC - 1)

    for d in (2, 1, 3):
        remote(act.at[:, r], act.at[:, r], a_s, a_r, (replica(d), e)).start()

    def returned(h, ch):
        arrived(rrecv.at[h, pl.ds(ch * KC, KC)], r_s.at[h], r_r.at[h * NC + ch])

    def combine(h):
        block = rrecv[h].reshape(NC * MROWS, MAIN)
        tsend[h, :, 0:MAIN] = dot(sel0[...], block, ((0,), (0,))).astype(BF16)
        tail = sum(dot(sel1[m], block[:, m * PIECE : (m + 1) * PIECE], ((0,), (0,))) for m in range(3))
        tsend[h, :, MAIN:HALF] = tail.astype(BF16)
        place = tok_out.at[:, pl.ds(pl.multiple_of(r * W + h * HALF, HALF), HALF)]

        def part(q):
            return tsend.at[h, pl.ds(pl.multiple_of(q * TOK, TOK), TOK)]

        pltpu.make_async_copy(part(r), place, t_r.at[h]).start()
        for d in (2, 1, 3):
            q = replica(d)
            remote(part(q), place, t_s.at[h], t_r.at[h], (q, e)).start()

    returned(0, 0)
    returned(0, 1)
    give_back(1, 1)
    returned(0, 2)
    give_back(1, 2)
    weight_grad(0, hid, win_out)
    returned(0, 3)
    give_back(1, 3)
    combine(0)
    arrived(act.at[:, pl.ds(0, 3)], a_s, a_r)
    weight_grad(1, act, wout_out)
    for ch in range(NC):
        returned(1, ch)
    combine(1)

    sent(pos_v.at[pl.ds(0, 3)], pos_s, pos_r)
    for a in range(2):
        for h in range(2):
            sent(xin.at[a, pl.ds(0, 3 * TOK), pl.ds(h * HALF, HALF)], x_s.at[a, h], x_r.at[a, h])
        sent(fsend.at[a, pl.ds(1, NE - 1)], f_s.at[a], f_r.at[0])
    sent(msend.at[pl.ds(0, 2)], m_s, m_r.at[0])
    sent(msend.at[0], fw_s, fw_r.at[0])
    sent(usend.at[pl.ds(0, 3)], u_s, u_r.at[0])
    sent(hid.at[pl.ds(0, 3)], h_s, h_r.at[0])
    sent(act.at[:, pl.ds(0, 3)], a_s, a_r)
    for h in range(2):
        sent(rsend.at[h, pl.ds(1, NE - 1)], r_s.at[h], r_r.at[h * NC])
        sent(tsend.at[h, pl.ds(0, 3 * TOK)], t_s.at[h], t_r.at[h])
    for h in range(2):
        arrived(tok_out.at[:, pl.ds(0, ND * HALF)], t_s.at[h], t_r.at[h])


def on_device(tokens, grad_out, gate_prob, expert_ids, w_in, w_out, threshold, spike_counts):
    vmem = pl.BlockSpec(memory_space=pltpu.VMEM)
    hbm = pl.BlockSpec(memory_space=pl.ANY)
    dma = pltpu.SemaphoreType.DMA
    out = pl.pallas_call(
        kernel,
        name="moe_backward",
        out_shape=(
            pltpu.VMEM((TOK, ND * W), BF16),
            pltpu.VMEM((W, FF), BF16),
            pltpu.VMEM((W, FF), BF16),
        ),
        in_specs=[vmem, vmem, vmem] + [hbm] * 5,
        out_specs=(vmem, vmem, vmem),
        scratch_shapes=[
            pltpu.VMEM((TOK, ND * W), BF16),
            pltpu.VMEM((TOK, ND * W), BF16),
            pltpu.VMEM((ROWS, FF), I32),
            pltpu.VMEM((W, FF), BF16),
            pltpu.VMEM((W, FF), BF16),
            pltpu.VMEM((ND, 8, TOK), I32),
            pltpu.VMEM((2, ND * TOK, W), BF16),
            pltpu.VMEM((NC * MROWS, ND * TOK), BF16),
            pltpu.VMEM((3, NC * MROWS, ND * TOK), BF16),
            pltpu.VMEM((ROWS, MROWS), BF16),
            pltpu.VMEM((3, ROWS, MROWS), BF16),
            pltpu.VMEM((MROWS, ROWS), BF16),
            pltpu.VMEM((3, MROWS, ROWS), BF16),
            pltpu.VMEM((2, NE, 2, 16, MAIN), BF16),
            pltpu.VMEM((2, NE, 2, 16, MAIN), BF16),
            pltpu.VMEM((2, NC * ROWS, W), BF16),
            pltpu.VMEM((NC, ND, HOME, FF), F32),
            pltpu.VMEM((NC, 2, 24, FF), F32),
            pltpu.VMEM((NC, 2, HOME, FF), F32),
            pltpu.VMEM((NC, ND, HOME, FF), F32),
            pltpu.VMEM((NC, ND, HOME, FF), BF16),
            pltpu.VMEM((NC, 3, HOME, FF), BF16),
            pltpu.VMEM((NC, ND, HOME, FF), BF16),
            pltpu.VMEM((NC, ND, HOME, FF), BF16),
            pltpu.VMEM((2, NE, 16, MAIN), BF16),
            pltpu.VMEM((2, NE, 16, MAIN), BF16),
            pltpu.VMEM((2, ND * TOK, HALF), BF16),
            dma((4,)),
            dma, dma,
            dma((2, 2)), dma((2, 2)),
            dma((2,)), dma((3 * NC,)),
            dma, dma((NC,)),
            dma, dma((NC,)),
            dma, dma((NC,)),
            dma, dma((NC,)),
            dma, dma,
            dma((2,)), dma((2 * NC,)),
            dma((2,)), dma((2,)),
        ],
        compiler_params=pltpu.CompilerParams(
            collective_id=0, has_side_effects=True, vmem_limit_bytes=52 << 20
        ),
        cost_estimate=pl.CostEstimate(flops=9 * 10**9, bytes_accessed=14 << 20, transcendentals=1 << 20),
    )(
        gate_prob.reshape(1, TOK), expert_ids.reshape(1, TOK), threshold, tokens, grad_out,
        w_in.reshape(W, FF), w_out.reshape(W, FF), spike_counts.reshape(ROWS, FF),
    )
    return out[0], out[1][None], out[2][None]


def solution(mesh):
    placed = (
        P(("dp", "expert"), None),
        P(("dp", "expert"), None),
        P(("dp", "expert")),
        P(("dp", "expert"), None),
        P("expert", "dp", None),
        P("expert", "dp", None),
        P("expert", None),
        P("expert", "dp", None),
    )
    return jax.shard_map(
        on_device,
        mesh=mesh,
        in_specs=placed,
        out_specs=(P(("dp", "expert"), None), P("expert", "dp", None), P("expert", "dp", None)),
        check_vma=False,
    )
```
